32 devices in a mesh: group: 2 (over y), blk: 8 (over z, x), layer: 2 (over core).
Axes of the slice: x: 2, y: 2, z: 4, core: 2. Of those that a mesh axis runs over, the one named last changes fastest.
Arguments:
- query_grads: bfloat16 [4096, 4, 4096], P(('group', 'blk'), 'layer'), parts along dimension 0, may hold values from -6 to 6
- train_grads: bfloat16 [64, 4, 4096], P(('group', 'blk'), 'layer'), parts along dimension 0, may hold values from -6 to 6
- basis_in: float32 [4, 64, 64], P('layer'), may hold values from -0.75 to 0.75
- basis_out: float32 [4, 64, 64], P('layer'), may hold values from -0.75 to 0.75
- eigen_in: float32 [4, 64], P('layer'), may hold values from 0.3 to 3
- eigen_out: float32 [4, 64], P('layer'), may hold values from 0.3 to 3
Outputs:
- influence: float32 [4096, 32], P(('group', 'blk'), 'layer'), parts along dimension 0
The draws below stay inside these ranges and needn't reach their ends.
There are 2 independent parts, one for each index of `group`. The reference program is written for one: setup_inputs(seed, part) draws one part's arguments, and reference() takes and returns one part's arrays. A program takes and returns all parts, laid end to end along the dimension named above; an argument that names none is the same for every part. Nothing has to cross between parts.
All inputs are finite; a program needn't handle non-finite values.
Results may differ from the reference program's by a relative error of at most 0.0029.
Values may be sent and summed in bfloat16 or wider, within the bound.
A program may use at most 128 MiB of HBM per device.

```python
import math
import jax
import jax.numpy as jnp
from jax import lax

RA = 64
RB = 64
PROJ = 4096
LAYERS = 4
QUERIES = 2048
TRAIN = 32


def block_levels(stream_key, dims, shards, low, high):
    def one(axis_at, blocks):
        draws = jax.random.uniform(jax.random.fold_in(jax.random.fold_in(stream_key, 6), axis_at), (blocks,), jnp.float32, low / len(shards), high / len(shards))
        return jnp.repeat(jnp.exp(draws), dims[axis_at] // blocks).reshape((-1,) + (1,) * (len(dims) - axis_at - 1))

    factor_of = one(*shards[0])
    for cut in shards[1:]:
        factor_of = factor_of * one(*cut)
    return factor_of


def centred(key, extent, deviation, most, pieces=(), held_as=jnp.bfloat16):
    gain = block_levels(key, extent, pieces, -0.22, 0.18) if pieces else 1.0
    array = jax.random.normal(key, extent, jnp.float32) * deviation * gain
    return jnp.minimum(jnp.maximum(array, -most), most).astype(held_as)


def setup_inputs(seed: int = 0, part: int = 0) -> dict:
    arg_keys = jax.random.split(jax.random.key(seed), 7)
    part_splits = jax.random.split(jax.random.fold_in(arg_keys[6], part), 7)
    return {
        "query_grads": centred(part_splits[0], (QUERIES, LAYERS, PROJ), 1.0, 6.0, ((0, 8), (1, 2))),
        "train_grads": centred(part_splits[1], (TRAIN, LAYERS, PROJ), 1.0, 6.0, ((0, 8), (1, 2))),
        "basis_in": centred(arg_keys[2], (LAYERS, RA, RA), RA ** -0.5, 0.75, ((0, 2),), jnp.float32),
        "basis_out": centred(arg_keys[3], (LAYERS, RB, RB), RB ** -0.5, 0.75, ((0, 2),), jnp.float32),
        "eigen_in": jnp.clip(jnp.exp(math.log(3.0) - 2.3025851 * jax.random.uniform(arg_keys[4], (LAYERS, RA), jnp.float32) ** block_levels(arg_keys[4], (LAYERS, RA), ((0, 2),), -0.2, 0.2)), 0.3, 3.0),
        "eigen_out": jnp.clip(jnp.exp(math.log(3.0) - 2.3025851 * jax.random.uniform(arg_keys[5], (LAYERS, RB), jnp.float32) ** block_levels(arg_keys[5], (LAYERS, RB), ((0, 2),), -0.2, 0.2)), 0.3, 3.0),
    }


def precondition_layer(grads, basis_a, basis_b, lam_a, lam_b):
    mats = grads.astype(jnp.float32).reshape(grads.shape[0], RA, RB)
    coef = jnp.einsum('ia,qib,bj->qaj', basis_a, mats, basis_b, precision=lax.Precision.HIGHEST)
    scaled = coef / (lam_a[:, None] * lam_b[None, :] + 0.1)
    back = jnp.einsum('ia,qaj,bj->qib', basis_a, scaled, basis_b, precision=lax.Precision.HIGHEST)
    return back.reshape(grads.shape[0], PROJ).astype(jnp.bfloat16)

def reference(query_grads, train_grads, basis_in, basis_out, eigen_in, eigen_out):

    def one_layer(total, index):
        query_layer = lax.dynamic_index_in_dim(query_grads, index, 1, keepdims=False)
        train_layer = lax.dynamic_index_in_dim(train_grads, index, 1, keepdims=False)
        precond = precondition_layer(query_layer, basis_in[index], basis_out[index], eigen_in[index], eigen_out[index])
        tile = lax.dot_general(precond, train_layer, (((1,), (1,)), ((), ())), preferred_element_type=jnp.float32)
        return (total + tile, None)
    start = jnp.zeros((QUERIES, TRAIN), jnp.float32)
    total, unused = lax.scan(one_layer, start, jnp.arange(LAYERS, dtype=jnp.int32))
    return total / jnp.sqrt(jnp.float32(LAYERS * PROJ))
```

```python
import jax
import jax.numpy as jnp
from jax import lax
from jax.experimental import pallas as pl
from jax.experimental.pallas import tpu as pltpu
from jax.sharding import PartitionSpec as P

RA = 64
RB = 64
MESH = pl.DeviceIdType.MESH
F32 = jnp.float32
BF16 = jnp.bfloat16


def split(x):
    high = x.astype(BF16)
    return high, (x - high.astype(F32)).astype(BF16)


def dot(a, b, dims):
    return lax.dot_general(a, b, (dims, ((), ())), preferred_element_type=F32)


def dot_wide(a, b, dims):
    ah, al = split(a)
    bh, bl = split(b)
    return dot(ah, bh, dims) + (dot(ah, bl, dims) + dot(al, bh, dims))


def kernel(n, scale, q_hbm, t_hbm, a_ref, b_ref, ei_ref, eo_ref, out_ref,
           qv, tv, wide, narrow, basis_pad, blocks, prod, part, other,
           q_sem, t_sem, send_sem, recv_sem, x_send, x_recv):
    group = lax.axis_index("group")
    me = lax.axis_index("blk")
    layer = lax.axis_index("layer")
    chunks = qv.shape[0]
    q_rows = qv.shape[1]
    t_rows = tv.shape[1]
    half = chunks // 2
    last = n // 2

    def block_at(pos):
        pos = lax.rem(pos + 2 * n, n)
        return jnp.where(pos < last, 2 * pos, 2 * (n - 1 - pos) + 1)

    pos = jnp.where(lax.rem(me, 2) == 0, me // 2, n - 1 - me // 2)
    right = (group, block_at(pos + 1), layer)
    left = (group, block_at(pos - 1), layer)
    partner = (group, me, 1 - layer)

    barrier = pltpu.get_barrier_semaphore()
    for device in (right, left, partner):
        pl.semaphore_signal(barrier, inc=1, device_id=device, device_id_type=MESH)

    def t_copy(c):
        return pltpu.make_async_copy(
            t_hbm.at[:, :, pl.ds(pl.multiple_of(c * 128, 128), 128)], tv.at[c], t_sem.at[c])

    def q_copy(c):
        return pltpu.make_async_copy(
            q_hbm.at[:, :, pl.ds(pl.multiple_of(c * 128, 128), 128)], qv.at[c], q_sem.at[c])

    @pl.loop(0, chunks)
    def _(c):
        t_copy(c).start()

    @pl.loop(0, chunks)
    def _(c):
        q_copy(c).start()

    b0, b1 = b_ref[0], b_ref[1]
    both = jnp.concatenate([b0, b1], axis=1)
    zero = jnp.zeros((RB, 128), F32)
    right_mat = jnp.concatenate(
        [jnp.concatenate([both, zero], axis=1), jnp.concatenate([zero, both], axis=1)], axis=0)

    @pl.loop(0, chunks)
    def _(c):
        t_copy(c).wait()

    rows = chunks * t_rows * 2
    t_all = tv[...].reshape(rows, 128)
    rh, rl = split(right_mat)
    turned = dot(t_all, rh, ((1,), (0,))) + dot(t_all, rl, ((1,), (0,)))
    for h in range(2):
        wide[h] = turned[:, h * 128:(h + 1) * 128]
    for l in range(2):
        basis_pad[l] = jnp.concatenate([a_ref[l], jnp.zeros((RA, 128 - RA), F32)], axis=1)

    eye = lax.broadcasted_iota(jnp.int32, (RA, RA), 0) == lax.broadcasted_iota(jnp.int32, (RA, RA), 1)
    step = 2 * t_rows
    for l in range(2):
        basis = jnp.concatenate(
            [basis_pad[l, pl.ds(h, RA // 2, stride=2), :] for h in range(2)], axis=0)[:, :RA]
        pieces = []
        for h in range(2):
            pieces.append(jnp.concatenate(
                [wide[h, pl.ds(2 * t + l, chunks, stride=step), :][:, l * 64:l * 64 + 64]
                 for t in range(t_rows)], axis=1))
        moved = jnp.concatenate(pieces, axis=0)
        coef = dot_wide(basis, moved, ((0,), (0,)))
        e_in = jnp.sum(jnp.where(eye, jnp.broadcast_to(ei_ref[l:l + 1, :], (RA, RA)), 0.0), axis=1, keepdims=True)
        denom = e_in * eo_ref[l:l + 1, :] + 0.1
        scaled = coef / jnp.concatenate([denom] * t_rows, axis=1)
        back = dot_wide(basis, scaled, ((1,), (0,)))
        for t in range(t_rows):
            narrow[pl.ds(2 * t + l, chunks, stride=step), :] = jnp.concatenate(
                [back[h * 32:(h + 1) * 32, t * 64:(t + 1) * 64] for h in range(2)], axis=1)

    zero_b = jnp.zeros((RB, RB), F32)
    left_mat = jnp.concatenate(
        [jnp.concatenate([b0, zero_b], axis=1), jnp.concatenate([zero_b, b0], axis=1),
         jnp.concatenate([b1, zero_b], axis=1), jnp.concatenate([zero_b, b1], axis=1)], axis=0)
    final = dot_wide(narrow[...], left_mat, ((1,), (1,)))
    parity = lax.rem(lax.broadcasted_iota(jnp.int32, (rows, 128), 0), 2)
    mine = jnp.where(parity == 0, final[:, :128], final[:, 128:])
    blocks[me] = mine.reshape(chunks, step, 128).astype(BF16)

    pl.semaphore_wait(barrier, 3)

    def hop(flow, d, side):
        owner = block_at(pos - d + 1 if flow == 0 else pos + d - 1)
        piece = blocks.at[owner, pl.ds(side * half, half)]
        return pltpu.make_async_remote_copy(
            src_ref=piece, dst_ref=piece,
            send_sem=send_sem.at[flow, d - 1, side], recv_sem=recv_sem.at[flow, d - 1, side],
            device_id=right if flow == 0 else left, device_id_type=MESH)

    def arrival(flow, d, side):
        owner = block_at(pos - d if flow == 0 else pos + d)
        piece = blocks.at[owner, pl.ds(side * half, half)]
        return pltpu.make_async_remote_copy(
            src_ref=piece, dst_ref=piece,
            send_sem=send_sem.at[flow, d - 1, side], recv_sem=recv_sem.at[flow, d - 1, side],
            device_id=right if flow == 0 else left, device_id_type=MESH)

    for side in range(2):
        for flow in range(2):
            hop(flow, 1, (side + flow) % 2).start()

    @pl.loop(1, last - 1)
    def _(d):
        for side in range(2):
            for flow in range(2):
                arrival(flow, d, (side + flow) % 2).wait_recv()
                hop(flow, d + 1, (side + flow) % 2).start()

    for flow in range(2):
        arrival(flow, last - 1, flow).wait_recv()
        hop(flow, last, flow).start()
    for flow in range(2):
        arrival(flow, last - 1, 1 - flow).wait_recv()

    @pl.loop(0, chunks)
    def _(c):
        q_copy(c).wait()

    for flow in range(2):
        arrival(flow, last, flow).wait_recv()

    total = None
    for c in range(0, chunks, 2):
        lhs = jnp.concatenate([qv[c + i].reshape(2 * q_rows, 128) for i in range(2)], axis=1)
        rhs = jnp.concatenate(
            [blocks[:, c + i].astype(F32).reshape(n * step, 128).astype(BF16) for i in range(2)], axis=1)
        term = dot(lhs, rhs, ((1,), (1,)))
        total = term if total is None else total + term
    columns = n * step
    tiles = prod.shape[0]
    if columns < tiles * 128:
        total = jnp.concatenate([total, jnp.zeros((2 * q_rows, tiles * 128 - columns), F32)], axis=1)
    for i in range(tiles):
        prod[i] = total[:, i * 128:(i + 1) * 128]

    def layer_rows(l):
        return jnp.concatenate(
            [prod[i, pl.ds(l, q_rows, stride=2), :].T for i in range(tiles)], axis=0)[:columns]

    first, second = layer_rows(0), layer_rows(1)
    odd = lax.rem(lax.broadcasted_iota(jnp.int32, (n * step, q_rows), 0), 2)
    prod_t = jnp.where(odd == 0, first, second)
    part_all = prod_t.reshape(n * t_rows, 2, q_rows).sum(axis=1) * scale
    part[...] = part_all.reshape(part.shape)

    swap = pltpu.make_async_remote_copy(
        src_ref=part.at[1 - layer], dst_ref=other, send_sem=x_send, recv_sem=x_recv,
        device_id=partner, device_id_type=MESH)
    swap.start()

    @pl.loop(1, last)
    def _(d):
        for side in range(2):
            for flow in range(2):
                hop(flow, d, side).wait_send()
    for flow in range(2):
        hop(flow, last, flow).wait_send()
    swap.wait()
    out_ref[...] = part[layer] + other[...]


def solution(mesh):
    n = mesh.shape["blk"]

    def shards(q, t, a, b, ei, eo):
        q_rows, _, width = q.shape
        t_rows = t.shape[0]
        chunks = width // 128
        scale = 1.0 / float((2 * mesh.shape["layer"] * width) ** 0.5)
        keep = n * t_rows // 2
        rows = chunks * t_rows * 2
        vmem = pl.BlockSpec(memory_space=pltpu.VMEM)
        hbm = pl.BlockSpec(memory_space=pl.ANY)
        out = pl.pallas_call(
            lambda *refs: kernel(n, scale, *refs),
            out_shape=jax.ShapeDtypeStruct((keep, q_rows), F32),
            in_specs=[hbm, hbm, vmem, vmem, vmem, vmem],
            out_specs=vmem,
            scratch_shapes=[
                pltpu.VMEM((chunks, q_rows, 2, 128), BF16),
                pltpu.VMEM((chunks, t_rows, 2, 128), BF16),
                pltpu.VMEM((2, rows, 128), F32),
                pltpu.VMEM((rows, 128), F32),
                pltpu.VMEM((2, RA, 128), F32),
                pltpu.VMEM((n, chunks, 2 * t_rows, 128), BF16),
                pltpu.VMEM((-(-n * t_rows * 2 // 128), 2 * q_rows, 128), F32),
                pltpu.VMEM((2, keep, q_rows), F32),
                pltpu.VMEM((keep, q_rows), F32),
                pltpu.SemaphoreType.DMA((chunks,)),
                pltpu.SemaphoreType.DMA((chunks,)),
                pltpu.SemaphoreType.DMA((2, n // 2, 2)),
                pltpu.SemaphoreType.DMA((2, n // 2, 2)),
                pltpu.SemaphoreType.DMA,
                pltpu.SemaphoreType.DMA,
            ],
            compiler_params=pltpu.CompilerParams(
                collective_id=0, has_side_effects=True, vmem_limit_bytes=56 * 2**20),
        )(q, t, a, b, ei, eo)
        return out.T

    placed = (
        P(("group", "blk"), "layer", None),
        P(("group", "blk"), "layer", None),
        P("layer", None, None),
        P("layer", None, None),
        P("layer", None),
        P("layer", None),
    )
    return jax.shard_map(
        shards, mesh=mesh, in_specs=placed, out_specs=P(("group", "blk"), "layer"), check_vma=False
    )
```

```python
import jax
import jax.numpy as jnp
from jax import lax
from jax.experimental import pallas as pl
from jax.experimental.pallas import tpu as pltpu
from jax.sharding import PartitionSpec as P

RA = 64
RB = 64
SIDES = 2
MESH = pl.DeviceIdType.MESH
F32 = jnp.float32
BF16 = jnp.bfloat16


def split(x):
    high = x.astype(BF16)
    return high, (x - high.astype(F32)).astype(BF16)


def dot(a, b, dims):
    return lax.dot_general(a, b, (dims, ((), ())), preferred_element_type=F32)


def dot_wide(a, b, dims):
    ah, al = split(a)
    bh, bl = split(b)
    return dot(ah, bh, dims) + (dot(ah, bl, dims) + dot(al, bh, dims))


def kernel(n, scale, q_hbm, t_hbm, a_ref, b_ref, ei_ref, eo_ref, out_ref,
           qv, tv, wide, narrow, basis_pad, blocks, prod, part, other,
           q_sem, t_sem, send_sem, recv_sem, x_send, x_recv):
    group = lax.axis_index("group")
    me = lax.axis_index("blk")
    layer = lax.axis_index("layer")
    chunks = qv.shape[0]
    q_rows = qv.shape[1]
    t_rows = tv.shape[1]

    line = n // 2
    across_at = me + 1 - 2 * lax.rem(me, 2)
    across = (group, across_at, layer)

    def peer(i):
        return (group, lax.rem(me + 2 * i, n), layer)

    partner = (group, me, 1 - layer)

    barrier = pltpu.get_barrier_semaphore()
    for device in (partner, across):
        pl.semaphore_signal(barrier, inc=1, device_id=device, device_id_type=MESH)

    @pl.loop(1, line)
    def _(i):
        pl.semaphore_signal(barrier, inc=1, device_id=peer(i), device_id_type=MESH)

    def t_copy(c):
        return pltpu.make_async_copy(
            t_hbm.at[:, :, pl.ds(pl.multiple_of(c * 128, 128), 128)], tv.at[c], t_sem.at[c])

    def q_copy(c):
        return pltpu.make_async_copy(
            q_hbm.at[:, :, pl.ds(pl.multiple_of(c * 128, 128), 128)], qv.at[c], q_sem.at[c])

    @pl.loop(0, chunks)
    def _(c):
        t_copy(c).start()

    @pl.loop(0, chunks)
    def _(c):
        q_copy(c).start()

    b0, b1 = b_ref[0], b_ref[1]
    both = jnp.concatenate([b0, b1], axis=1)
    zero = jnp.zeros((RB, 128), F32)
    right_mat = jnp.concatenate(
        [jnp.concatenate([both, zero], axis=1), jnp.concatenate([zero, both], axis=1)], axis=0)

    @pl.loop(0, chunks)
    def _(c):
        t_copy(c).wait()

    rows = chunks * t_rows * 2
    t_all = tv[...].reshape(rows, 128)
    rh, rl = split(right_mat)
    turned = dot(t_all, rh, ((1,), (0,))) + dot(t_all, rl, ((1,), (0,)))
    for h in range(2):
        wide[h] = turned[:, h * 128:(h + 1) * 128]
    for l in range(2):
        basis_pad[l] = jnp.concatenate([a_ref[l], jnp.zeros((RA, 128 - RA), F32)], axis=1)

    eye = lax.broadcasted_iota(jnp.int32, (RA, RA), 0) == lax.broadcasted_iota(jnp.int32, (RA, RA), 1)
    step = 2 * t_rows
    for l in range(2):
        basis = jnp.concatenate(
            [basis_pad[l, pl.ds(h, RA // 2, stride=2), :] for h in range(2)], axis=0)[:, :RA]
        pieces = []
        for h in range(2):
            pieces.append(jnp.concatenate(
                [wide[h, pl.ds(2 * t + l, chunks, stride=step), :][:, l * 64:l * 64 + 64]
                 for t in range(t_rows)], axis=1))
        moved = jnp.concatenate(pieces, axis=0)
        coef = dot_wide(basis, moved, ((0,), (0,)))
        e_in = jnp.sum(jnp.where(eye, jnp.broadcast_to(ei_ref[l:l + 1, :], (RA, RA)), 0.0), axis=1, keepdims=True)
        denom = e_in * eo_ref[l:l + 1, :] + 0.1
        scaled = coef / jnp.concatenate([denom] * t_rows, axis=1)
        back = dot_wide(basis, scaled, ((1,), (0,)))
        for t in range(t_rows):
            narrow[pl.ds(2 * t + l, chunks, stride=step), :] = jnp.concatenate(
                [back[h * 32:(h + 1) * 32, t * 64:(t + 1) * 64] for h in range(2)], axis=1)

    zero_b = jnp.zeros((RB, RB), F32)
    left_mat = jnp.concatenate(
        [jnp.concatenate([b0, zero_b], axis=1), jnp.concatenate([zero_b, b0], axis=1),
         jnp.concatenate([b1, zero_b], axis=1), jnp.concatenate([zero_b, b1], axis=1)], axis=0)
    final = dot_wide(narrow[...], left_mat, ((1,), (1,)))
    parity = lax.rem(lax.broadcasted_iota(jnp.int32, (rows, 128), 0), 2)
    mine = jnp.where(parity == 0, final[:, :128], final[:, 128:])
    blocks[me] = mine.reshape(chunks, step, 128).astype(BF16)

    pl.semaphore_wait(barrier, line + 1)

    span = chunks // SIDES

    def along(i, owner, side):
        piece = blocks.at[owner, pl.ds(side * span, span)]
        return pltpu.make_async_remote_copy(
            src_ref=piece, dst_ref=piece,
            send_sem=send_sem.at[side, i], recv_sem=recv_sem.at[side, i],
            device_id=peer(i), device_id_type=MESH)

    def over(i, owner, side):
        piece = blocks.at[owner, pl.ds(side * span, span)]
        return pltpu.make_async_remote_copy(
            src_ref=piece, dst_ref=piece,
            send_sem=send_sem.at[side, line + i], recv_sem=recv_sem.at[side, line + i],
            device_id=across, device_id_type=MESH)

    def source(base, i):
        return lax.rem(base + n - 2 * i, n)

    for side in range(SIDES):
        over(0, me, side).start()

        @pl.loop(1, line)
        def _(i):
            along(i, me, side).start()

    for side in range(SIDES):
        @pl.loop(1, line)
        def _(i):
            along(i, source(me, i), side).wait_recv()
            over(i, source(me, i), side).start()

    @pl.loop(0, chunks)
    def _(c):
        q_copy(c).wait()

    total = None
    for c in range(0, chunks, 2):
        if c % span == 0:
            @pl.loop(0, line)
            def _(i):
                over(i, source(across_at, i), c // span).wait_recv()

        lhs = jnp.concatenate([qv[c + i].reshape(2 * q_rows, 128) for i in range(2)], axis=1)
        rhs = jnp.concatenate(
            [blocks[:, c + i].astype(F32).reshape(n * step, 128).astype(BF16) for i in range(2)], axis=1)
        term = dot(lhs, rhs, ((1,), (1,)))
        total = term if total is None else total + term
    columns = n * step
    tiles = prod.shape[0]
    if columns < tiles * 128:
        total = jnp.concatenate([total, jnp.zeros((2 * q_rows, tiles * 128 - columns), F32)], axis=1)
    for i in range(tiles):
        prod[i] = total[:, i * 128:(i + 1) * 128]

    def layer_rows(l):
        return jnp.concatenate(
            [prod[i, pl.ds(l, q_rows, stride=2), :].T for i in range(tiles)], axis=0)[:columns]

    first, second = layer_rows(0), layer_rows(1)
    odd = lax.rem(lax.broadcasted_iota(jnp.int32, (n * step, q_rows), 0), 2)
    prod_t = jnp.where(odd == 0, first, second)
    part_all = prod_t.reshape(n * t_rows, 2, q_rows).sum(axis=1) * scale
    part[...] = part_all.reshape(part.shape)

    swap = pltpu.make_async_remote_copy(
        src_ref=part.at[1 - layer], dst_ref=other, send_sem=x_send, recv_sem=x_recv,
        device_id=partner, device_id_type=MESH)
    swap.start()

    for side in range(SIDES):
        over(0, me, side).wait_send()

        @pl.loop(1, line)
        def _(i):
            along(i, me, side).wait_send()
            over(i, source(me, i), side).wait_send()
    swap.wait()
    out_ref[...] = part[layer] + other[...]


def solution(mesh):
    n = mesh.shape["blk"]

    def shards(q, t, a, b, ei, eo):
        q_rows, _, width = q.shape
        t_rows = t.shape[0]
        chunks = width // 128
        scale = 1.0 / float((2 * mesh.shape["layer"] * width) ** 0.5)
        keep = n * t_rows // 2
        rows = chunks * t_rows * 2
        vmem = pl.BlockSpec(memory_space=pltpu.VMEM)
        hbm = pl.BlockSpec(memory_space=pl.ANY)
        out = pl.pallas_call(
            lambda *refs: kernel(n, scale, *refs),
            out_shape=jax.ShapeDtypeStruct((keep, q_rows), F32),
            in_specs=[hbm, hbm, vmem, vmem, vmem, vmem],
            out_specs=vmem,
            scratch_shapes=[
                pltpu.VMEM((chunks, q_rows, 2, 128), BF16),
                pltpu.VMEM((chunks, t_rows, 2, 128), BF16),
                pltpu.VMEM((2, rows, 128), F32),
                pltpu.VMEM((rows, 128), F32),
                pltpu.VMEM((2, RA, 128), F32),
                pltpu.VMEM((n, chunks, 2 * t_rows, 128), BF16),
                pltpu.VMEM((-(-n * t_rows * 2 // 128), 2 * q_rows, 128), F32),
                pltpu.VMEM((2, keep, q_rows), F32),
                pltpu.VMEM((keep, q_rows), F32),
                pltpu.SemaphoreType.DMA((chunks,)),
                pltpu.SemaphoreType.DMA((chunks,)),
                pltpu.SemaphoreType.DMA((SIDES, n)),
                pltpu.SemaphoreType.DMA((SIDES, n)),
                pltpu.SemaphoreType.DMA,
                pltpu.SemaphoreType.DMA,
            ],
            compiler_params=pltpu.CompilerParams(
                collective_id=0, has_side_effects=True, vmem_limit_bytes=56 * 2**20),
        )(q, t, a, b, ei, eo)
        return out.T

    placed = (
        P(("group", "blk"), "layer", None),
        P(("group", "blk"), "layer", None),
        P("layer", None, None),
        P("layer", None, None),
        P("layer", None),
        P("layer", None),
    )
    return jax.shard_map(
        shards, mesh=mesh, in_specs=placed, out_specs=P(("group", "blk"), "layer"), check_vma=False
    )
```

```python
import jax
import jax.numpy as jnp
from jax import lax
from jax.experimental import pallas as pl
from jax.experimental.pallas import tpu as pltpu
from jax.sharding import PartitionSpec as P

RA = 64
RB = 64
SIDES = 2
MESH = pl.DeviceIdType.MESH
F32 = jnp.float32
BF16 = jnp.bfloat16


def split(x):
    high = x.astype(BF16)
    return high, (x - high.astype(F32)).astype(BF16)


def dot(a, b, dims):
    return lax.dot_general(a, b, (dims, ((), ())), preferred_element_type=F32)


def dot_wide(a, b, dims):
    ah, al = split(a)
    bh, bl = split(b)
    return dot(ah, bh, dims) + (dot(ah, bl, dims) + dot(al, bh, dims))


def kernel(n, scale, q_hbm, t_hbm, a_ref, b_ref, ei_ref, eo_ref, out_ref,
           qv, tv, wide, narrow, basis_pad, blocks, prod, part, other,
           q_sem, t_sem, send_sem, recv_sem, x_send, x_recv):
    group = lax.axis_index("group")
    me = lax.axis_index("blk")
    layer = lax.axis_index("layer")
    chunks = qv.shape[0]
    q_rows = qv.shape[1]
    t_rows = tv.shape[1]

    line = n // 2
    across_at = me + 1 - 2 * lax.rem(me, 2)
    across = (group, across_at, layer)

    def peer(i):
        return (group, lax.rem(me + 2 * i, n), layer)

    partner = (group, me, 1 - layer)

    barrier = pltpu.get_barrier_semaphore()
    for device in (partner, across):
        pl.semaphore_signal(barrier, inc=1, device_id=device, device_id_type=MESH)

    @pl.loop(1, line)
    def _(i):
        pl.semaphore_signal(barrier, inc=1, device_id=peer(i), device_id_type=MESH)

    def t_copy(c):
        return pltpu.make_async_copy(
            t_hbm.at[:, :, pl.ds(pl.multiple_of(c * 128, 128), 128)], tv.at[c], t_sem.at[c])

    def q_copy(c):
        return pltpu.make_async_copy(
            q_hbm.at[:, :, pl.ds(pl.multiple_of(c * 128, 128), 128)], qv.at[c], q_sem.at[c])

    @pl.loop(0, chunks)
    def _(c):
        t_copy(c).start()

    b0, b1 = b_ref[0], b_ref[1]
    both = jnp.concatenate([b0, b1], axis=1)
    zero = jnp.zeros((RB, 128), F32)
    right_mat = jnp.concatenate(
        [jnp.concatenate([both, zero], axis=1), jnp.concatenate([zero, both], axis=1)], axis=0)

    @pl.loop(0, chunks)
    def _(c):
        t_copy(c).wait()

    rows = chunks * t_rows * 2
    t_all = tv[...].reshape(rows, 128)
    rh, rl = split(right_mat)
    turned = dot(t_all, rh, ((1,), (0,))) + dot(t_all, rl, ((1,), (0,)))
    for h in range(2):
        wide[h] = turned[:, h * 128:(h + 1) * 128]
    for l in range(2):
        basis_pad[l] = jnp.concatenate([a_ref[l], jnp.zeros((RA, 128 - RA), F32)], axis=1)

    eye = lax.broadcasted_iota(jnp.int32, (RA, RA), 0) == lax.broadcasted_iota(jnp.int32, (RA, RA), 1)
    step = 2 * t_rows
    for l in range(2):
        basis = jnp.concatenate(
            [basis_pad[l, pl.ds(h, RA // 2, stride=2), :] for h in range(2)], axis=0)[:, :RA]
        pieces = []
        for h in range(2):
            pieces.append(jnp.concatenate(
                [wide[h, pl.ds(2 * t + l, chunks, stride=step), :][:, l * 64:l * 64 + 64]
                 for t in range(t_rows)], axis=1))
        moved = jnp.concatenate(pieces, axis=0)
        coef = dot_wide(basis, moved, ((0,), (0,)))
        e_in = jnp.sum(jnp.where(eye, jnp.broadcast_to(ei_ref[l:l + 1, :], (RA, RA)), 0.0), axis=1, keepdims=True)
        denom = e_in * eo_ref[l:l + 1, :] + 0.1
        scaled = coef / jnp.concatenate([denom] * t_rows, axis=1)
        back = dot_wide(basis, scaled, ((1,), (0,)))
        for t in range(t_rows):
            narrow[pl.ds(2 * t + l, chunks, stride=step), :] = jnp.concatenate(
                [back[h * 32:(h + 1) * 32, t * 64:(t + 1) * 64] for h in range(2)], axis=1)

    zero_b = jnp.zeros((RB, RB), F32)
    left_mat = jnp.concatenate(
        [jnp.concatenate([b0, zero_b], axis=1), jnp.concatenate([zero_b, b0], axis=1),
         jnp.concatenate([b1, zero_b], axis=1), jnp.concatenate([zero_b, b1], axis=1)], axis=0)
    final = dot_wide(narrow[...], left_mat, ((1,), (1,)))
    parity = lax.rem(lax.broadcasted_iota(jnp.int32, (rows, 128), 0), 2)
    mine = jnp.where(parity == 0, final[:, :128], final[:, 128:])
    blocks[me] = mine.reshape(chunks, step, 128).astype(BF16)

    pl.semaphore_wait(barrier, line + 1)

    span = chunks // SIDES

    def along(i, owner, side):
        piece = blocks.at[owner, pl.ds(side * span, span)]
        return pltpu.make_async_remote_copy(
            src_ref=piece, dst_ref=piece,
            send_sem=send_sem.at[side, i], recv_sem=recv_sem.at[side, i],
            device_id=peer(i), device_id_type=MESH)

    def over(i, owner, side):
        piece = blocks.at[owner, pl.ds(side * span, span)]
        return pltpu.make_async_remote_copy(
            src_ref=piece, dst_ref=piece,
            send_sem=send_sem.at[side, line + i], recv_sem=recv_sem.at[side, line + i],
            device_id=across, device_id_type=MESH)

    def source(base, i):
        return lax.rem(base + n - 2 * i, n)

    for side in range(SIDES):
        over(0, me, side).start()

        @pl.loop(1, line)
        def _(i):
            along(i, me, side).start()

    @pl.loop(0, chunks)
    def _(c):
        q_copy(c).start()

    for side in range(SIDES):
        @pl.loop(1, line)
        def _(i):
            along(i, source(me, i), side).wait_recv()
            over(i, source(me, i), side).start()

    @pl.loop(0, chunks)
    def _(c):
        q_copy(c).wait()

    total = None
    for c in range(0, chunks, 2):
        if c % span == 0:
            @pl.loop(0, line)
            def _(i):
                over(i, source(across_at, i), c // span).wait_recv()

        lhs = jnp.concatenate([qv[c + i].reshape(2 * q_rows, 128) for i in range(2)], axis=1)
        rhs = jnp.concatenate(
            [blocks[:, c + i].astype(F32).reshape(n * step, 128).astype(BF16) for i in range(2)], axis=1)
        term = dot(lhs, rhs, ((1,), (1,)))
        total = term if total is None else total + term
    columns = n * step
    tiles = prod.shape[0]
    if columns < tiles * 128:
        total = jnp.concatenate([total, jnp.zeros((2 * q_rows, tiles * 128 - columns), F32)], axis=1)
    for i in range(tiles):
        prod[i] = total[:, i * 128:(i + 1) * 128]

    def layer_rows(l):
        return jnp.concatenate(
            [prod[i, pl.ds(l, q_rows, stride=2), :].T for i in range(tiles)], axis=0)[:columns]

    first, second = layer_rows(0), layer_rows(1)
    odd = lax.rem(lax.broadcasted_iota(jnp.int32, (n * step, q_rows), 0), 2)
    prod_t = jnp.where(odd == 0, first, second)
    part_all = prod_t.reshape(n * t_rows, 2, q_rows).sum(axis=1) * scale
    part[...] = part_all.reshape(part.shape)

    swap = pltpu.make_async_remote_copy(
        src_ref=part.at[1 - layer], dst_ref=other, send_sem=x_send, recv_sem=x_recv,
        device_id=partner, device_id_type=MESH)
    swap.start()

    for side in range(SIDES):
        over(0, me, side).wait_send()

        @pl.loop(1, line)
        def _(i):
            along(i, me, side).wait_send()
            over(i, source(me, i), side).wait_send()
    swap.wait()
    out_ref[...] = part[layer] + other[...]


def solution(mesh):
    n = mesh.shape["blk"]

    def shards(q, t, a, b, ei, eo):
        q_rows, _, width = q.shape
        t_rows = t.shape[0]
        chunks = width // 128
        scale = 1.0 / float((2 * mesh.shape["layer"] * width) ** 0.5)
        keep = n * t_rows // 2
        rows = chunks * t_rows * 2
        vmem = pl.BlockSpec(memory_space=pltpu.VMEM)
        hbm = pl.BlockSpec(memory_space=pl.ANY)
        out = pl.pallas_call(
            lambda *refs: kernel(n, scale, *refs),
            out_shape=jax.ShapeDtypeStruct((keep, q_rows), F32),
            in_specs=[hbm, hbm, vmem, vmem, vmem, vmem],
            out_specs=vmem,
            scratch_shapes=[
                pltpu.VMEM((chunks, q_rows, 2, 128), BF16),
                pltpu.VMEM((chunks, t_rows, 2, 128), BF16),
                pltpu.VMEM((2, rows, 128), F32),
                pltpu.VMEM((rows, 128), F32),
                pltpu.VMEM((2, RA, 128), F32),
                pltpu.VMEM((n, chunks, 2 * t_rows, 128), BF16),
                pltpu.VMEM((-(-n * t_rows * 2 // 128), 2 * q_rows, 128), F32),
                pltpu.VMEM((2, keep, q_rows), F32),
                pltpu.VMEM((keep, q_rows), F32),
                pltpu.SemaphoreType.DMA((chunks,)),
                pltpu.SemaphoreType.DMA((chunks,)),
                pltpu.SemaphoreType.DMA((SIDES, n)),
                pltpu.SemaphoreType.DMA((SIDES, n)),
                pltpu.SemaphoreType.DMA,
                pltpu.SemaphoreType.DMA,
            ],
            compiler_params=pltpu.CompilerParams(
                collective_id=0, has_side_effects=True, vmem_limit_bytes=56 * 2**20),
        )(q, t, a, b, ei, eo)
        return out.T

    placed = (
        P(("group", "blk"), "layer", None),
        P(("group", "blk"), "layer", None),
        P("layer", None, None),
        P("layer", None, None),
        P("layer", None),
        P("layer", None),
    )
    return jax.shard_map(
        shards, mesh=mesh, in_specs=placed, out_specs=P(("group", "blk"), "layer"), check_vma=False
    )
```

```python
import jax
import jax.numpy as jnp
from jax import lax
from jax.experimental import pallas as pl
from jax.experimental.pallas import tpu as pltpu
from jax.sharding import PartitionSpec as P

RA = 64
RB = 64
SIDES = 2
MESH = pl.DeviceIdType.MESH
F32 = jnp.float32
BF16 = jnp.bfloat16


def split(x):
    high = x.astype(BF16)
    return high, (x - high.astype(F32)).astype(BF16)


def dot(a, b, dims):
    return lax.dot_general(a, b, (dims, ((), ())), preferred_element_type=F32)


def dot_wide(a, b, dims):
    ah, al = split(a)
    bh, bl = split(b)
    return dot(ah, bh, dims) + (dot(ah, bl, dims) + dot(al, bh, dims))


def kernel(n, scale, q_hbm, t_hbm, a_ref, b_ref, ei_ref, eo_ref, out_ref,
           qv, tv, wide, narrow, basis_pad, blocks, prod, part, other,
           q_sem, t_sem, send_sem, recv_sem, x_send, x_recv):
    group = lax.axis_index("group")
    me = lax.axis_index("blk")
    layer = lax.axis_index("layer")
    chunks = qv.shape[0]
    q_rows = qv.shape[1]
    t_rows = tv.shape[1]

    line = n // 2
    across_at = me + 1 - 2 * lax.rem(me, 2)
    across = (group, across_at, layer)

    def peer(i):
        return (group, lax.rem(me + 2 * i, n), layer)

    partner = (group, me, 1 - layer)

    barrier = pltpu.get_barrier_semaphore()
    for device in (partner, across):
        pl.semaphore_signal(barrier, inc=1, device_id=device, device_id_type=MESH)

    @pl.loop(1, line)
    def _(i):
        pl.semaphore_signal(barrier, inc=1, device_id=peer(i), device_id_type=MESH)

    def t_copy(c):
        return pltpu.make_async_copy(
            t_hbm.at[:, :, pl.ds(pl.multiple_of(c * 128, 128), 128)], tv.at[c], t_sem.at[c])

    def q_copy(c):
        return pltpu.make_async_copy(
            q_hbm.at[:, :, pl.ds(pl.multiple_of(c * 128, 128), 128)], qv.at[c], q_sem.at[c])

    @pl.loop(0, chunks, unroll=8)
    def _(c):
        t_copy(c).start()

    b0, b1 = b_ref[0], b_ref[1]
    both = jnp.concatenate([b0, b1], axis=1)
    zero = jnp.zeros((RB, 128), F32)
    right_mat = jnp.concatenate(
        [jnp.concatenate([both, zero], axis=1), jnp.concatenate([zero, both], axis=1)], axis=0)

    @pl.loop(0, chunks, unroll=8)
    def _(c):
        t_copy(c).wait()

    rows = chunks * t_rows * 2
    t_all = tv[...].reshape(rows, 128)
    rh, rl = split(right_mat)
    turned = dot(t_all, rh, ((1,), (0,))) + dot(t_all, rl, ((1,), (0,)))
    for h in range(2):
        wide[h] = turned[:, h * 128:(h + 1) * 128]
    for l in range(2):
        basis_pad[l] = jnp.concatenate([a_ref[l], jnp.zeros((RA, 128 - RA), F32)], axis=1)

    eye = lax.broadcasted_iota(jnp.int32, (RA, RA), 0) == lax.broadcasted_iota(jnp.int32, (RA, RA), 1)
    step = 2 * t_rows
    for l in range(2):
        basis = jnp.concatenate(
            [basis_pad[l, pl.ds(h, RA // 2, stride=2), :] for h in range(2)], axis=0)[:, :RA]
        pieces = []
        for h in range(2):
            pieces.append(jnp.concatenate(
                [wide[h, pl.ds(2 * t + l, chunks, stride=step), :][:, l * 64:l * 64 + 64]
                 for t in range(t_rows)], axis=1))
        moved = jnp.concatenate(pieces, axis=0)
        coef = dot_wide(basis, moved, ((0,), (0,)))
        e_in = jnp.sum(jnp.where(eye, jnp.broadcast_to(ei_ref[l:l + 1, :], (RA, RA)), 0.0), axis=1, keepdims=True)
        denom = e_in * eo_ref[l:l + 1, :] + 0.1
        scaled = coef / jnp.concatenate([denom] * t_rows, axis=1)
        back = dot_wide(basis, scaled, ((1,), (0,)))
        for t in range(t_rows):
            narrow[pl.ds(2 * t + l, chunks, stride=step), :] = jnp.concatenate(
                [back[h * 32:(h + 1) * 32, t * 64:(t + 1) * 64] for h in range(2)], axis=1)

    zero_b = jnp.zeros((RB, RB), F32)
    left_mat = jnp.concatenate(
        [jnp.concatenate([b0, zero_b], axis=1), jnp.concatenate([zero_b, b0], axis=1),
         jnp.concatenate([b1, zero_b], axis=1), jnp.concatenate([zero_b, b1], axis=1)], axis=0)
    final = dot_wide(narrow[...], left_mat, ((1,), (1,)))
    parity = lax.rem(lax.broadcasted_iota(jnp.int32, (rows, 128), 0), 2)
    mine = jnp.where(parity == 0, final[:, :128], final[:, 128:])
    blocks[me] = mine.reshape(chunks, step, 128).astype(BF16)

    pl.semaphore_wait(barrier, line + 1)

    span = chunks // SIDES

    def along(i, owner, side):
        piece = blocks.at[owner, pl.ds(side * span, span)]
        return pltpu.make_async_remote_copy(
            src_ref=piece, dst_ref=piece,
            send_sem=send_sem.at[side, i], recv_sem=recv_sem.at[side, i],
            device_id=peer(i), device_id_type=MESH)

    def over(i, owner, side):
        piece = blocks.at[owner, pl.ds(side * span, span)]
        return pltpu.make_async_remote_copy(
            src_ref=piece, dst_ref=piece,
            send_sem=send_sem.at[side, line + i], recv_sem=recv_sem.at[side, line + i],
            device_id=across, device_id_type=MESH)

    def source(base, i):
        return lax.rem(base + n - 2 * i, n)

    for side in range(SIDES):
        over(0, me, side).start()

        @pl.loop(1, line)
        def _(i):
            along(i, me, side).start()

    @pl.loop(0, chunks)
    def _(c):
        q_copy(c).start()

    for side in range(SIDES):
        @pl.loop(1, line)
        def _(i):
            along(i, source(me, i), side).wait_recv()
            over(i, source(me, i), side).start()

    @pl.loop(0, chunks)
    def _(c):
        q_copy(c).wait()

    total = None
    for c in range(0, chunks, 2):
        if c % span == 0:
            @pl.loop(0, line)
            def _(i):
                over(i, source(across_at, i), c // span).wait_recv()

        lhs = jnp.concatenate([qv[c + i].reshape(2 * q_rows, 128) for i in range(2)], axis=1)
        rhs = jnp.concatenate(
            [blocks[:, c + i].astype(F32).reshape(n * step, 128).astype(BF16) for i in range(2)], axis=1)
        term = dot(lhs, rhs, ((1,), (1,)))
        total = term if total is None else total + term
    columns = n * step
    tiles = prod.shape[0]
    if columns < tiles * 128:
        total = jnp.concatenate([total, jnp.zeros((2 * q_rows, tiles * 128 - columns), F32)], axis=1)
    for i in range(tiles):
        prod[i] = total[:, i * 128:(i + 1) * 128]

    def layer_rows(l):
        return jnp.concatenate(
            [prod[i, pl.ds(l, q_rows, stride=2), :].T for i in range(tiles)], axis=0)[:columns]

    first, second = layer_rows(0), layer_rows(1)
    odd = lax.rem(lax.broadcasted_iota(jnp.int32, (n * step, q_rows), 0), 2)
    prod_t = jnp.where(odd == 0, first, second)
    part_all = prod_t.reshape(n * t_rows, 2, q_rows).sum(axis=1) * scale
    part[...] = part_all.reshape(part.shape)

    swap = pltpu.make_async_remote_copy(
        src_ref=part.at[1 - layer], dst_ref=other, send_sem=x_send, recv_sem=x_recv,
        device_id=partner, device_id_type=MESH)
    swap.start()

    for side in range(SIDES):
        over(0, me, side).wait_send()

        @pl.loop(1, line)
        def _(i):
            along(i, me, side).wait_send()
            over(i, source(me, i), side).wait_send()
    swap.wait()
    out_ref[...] = part[layer] + other[...]


def solution(mesh):
    n = mesh.shape["blk"]

    def shards(q, t, a, b, ei, eo):
        q_rows, _, width = q.shape
        t_rows = t.shape[0]
        chunks = width // 128
        scale = 1.0 / float((2 * mesh.shape["layer"] * width) ** 0.5)
        keep = n * t_rows // 2
        rows = chunks * t_rows * 2
        vmem = pl.BlockSpec(memory_space=pltpu.VMEM)
        hbm = pl.BlockSpec(memory_space=pl.ANY)
        out = pl.pallas_call(
            lambda *refs: kernel(n, scale, *refs),
            out_shape=jax.ShapeDtypeStruct((keep, q_rows), F32),
            in_specs=[hbm, hbm, vmem, vmem, vmem, vmem],
            out_specs=vmem,
            scratch_shapes=[
                pltpu.VMEM((chunks, q_rows, 2, 128), BF16),
                pltpu.VMEM((chunks, t_rows, 2, 128), BF16),
                pltpu.VMEM((2, rows, 128), F32),
                pltpu.VMEM((rows, 128), F32),
                pltpu.VMEM((2, RA, 128), F32),
                pltpu.VMEM((n, chunks, 2 * t_rows, 128), BF16),
                pltpu.VMEM((-(-n * t_rows * 2 // 128), 2 * q_rows, 128), F32),
                pltpu.VMEM((2, keep, q_rows), F32),
                pltpu.VMEM((keep, q_rows), F32),
                pltpu.SemaphoreType.DMA((chunks,)),
                pltpu.SemaphoreType.DMA((chunks,)),
                pltpu.SemaphoreType.DMA((SIDES, n)),
                pltpu.SemaphoreType.DMA((SIDES, n)),
                pltpu.SemaphoreType.DMA,
                pltpu.SemaphoreType.DMA,
            ],
            compiler_params=pltpu.CompilerParams(
                collective_id=0, has_side_effects=True, vmem_limit_bytes=56 * 2**20),
        )(q, t, a, b, ei, eo)
        return out.T

    placed = (
        P(("group", "blk"), "layer", None),
        P(("group", "blk"), "layer", None),
        P("layer", None, None),
        P("layer", None, None),
        P("layer", None),
        P("layer", None),
    )
    return jax.shard_map(
        shards, mesh=mesh, in_specs=placed, out_specs=P(("group", "blk"), "layer"), check_vma=False
    )
```
